128 devices in a mesh: replica: 2 (over core), fsdp: 64 (over z, y, x).
Axes of the slice: x: 4, y: 4, z: 4, core: 2. Of those that a mesh axis runs over, the one named last changes fastest.
Arguments:
- partials: bfloat16 [2, 512, 131072], P('replica', 'fsdp'), may hold values from -30 to 30
- owners: int32 [2, 128, 1], replicated, may hold values from 0 to 63; in each aligned block of 128 rows (0 to 127, 128 to 255, ..., all dimensions but the last counted through in order) at most 3 rows name the same one
- left_stat: float32 [384, 512, 512], P(('replica', 'fsdp')), may hold values from -1 to 6
- right_stat: float32 [384, 512, 512], P(('replica', 'fsdp')), may hold values from -1 to 6
- left_root: bfloat16 [384, 512, 512], P(('replica', 'fsdp')), may hold values from -0.5 to 3.5
- right_root: bfloat16 [384, 512, 512], P(('replica', 'fsdp')), may hold values from -0.5 to 3.5
- second_moment: float32 [384, 512, 512], P(('replica', 'fsdp')), may hold values from 0.1 to 3
Outputs:
- left_next: float32 [384, 512, 512], P(('replica', 'fsdp'))
- right_next: float32 [384, 512, 512], P(('replica', 'fsdp'))
- moment_next: float32 [384, 512, 512], P(('replica', 'fsdp'))
- update: bfloat16 [512, 131072], P('fsdp', 'replica')
The draws below stay inside these ranges and needn't reach their ends.
Inputs may be any that keep to these rules, and one draw needn't show every extreme that they name: In each column half h, no fsdp index is named by more than 3 of the 128 entries owners[h], a bound that some block reaches.
All inputs are finite; a program needn't handle non-finite values.
Results may differ from the reference program's by a relative error of at most 0.012.
Values may be sent and summed in bfloat16 or wider, within the bound.
No kernel may reach another device: no remote copies, remote signals or barrier semaphores. Data moves between devices by JAX's collectives and lax.ppermute only.
A program may use at most 128 MiB of HBM per device.

```python
import math
import jax
import jax.numpy as jnp
import numpy as np
from jax import lax

B = 512
SLOTS = 3
NBH = 128
NB = 256
C = 131072
NS = 384
N_REPLICA = 2
N_FSDP = 64


def symmetrize(noise, diagonal, spread):
    order_index = jnp.arange(B)
    identity = (order_index[:, None] == order_index[None, :]).astype(jnp.float32)
    return (noise + jnp.swapaxes(noise, 1, 2)) * (0.5 * spread) + diagonal[:, :, None] * identity[None, :, :]


def draw_factor(key, diag_lo, diag_hi, spread):
    first, second = jax.random.split(key)
    noise = jax.random.normal(first, (NS, B, B), jnp.float32)
    diagonal = jnp.exp(jax.random.uniform(second, (NS, B), jnp.float32, math.log(diag_lo), math.log(diag_hi)))
    return symmetrize(noise, diagonal, spread)


def draw_partials(key, part):
    key = jax.random.fold_in(key, 3)
    first, second, third = jax.random.split(key, 3)
    row_scale = jnp.exp(jax.random.uniform(second, (B,), jnp.float32, 0.0, math.log(10.0))) / math.sqrt(10.0)
    column_scale = jnp.exp(jax.random.uniform(third, (C,), jnp.float32, 0.0, math.log(10.0))) / math.sqrt(10.0)
    noise = jnp.clip(jax.random.normal(first, (N_REPLICA, B, C), jnp.float32), -6.0, 6.0)
    return (0.5 * noise * row_scale[None, :, None] * column_scale[None, None, :]).astype(jnp.bfloat16)


def draw_left_stat(key, part):
    key = jax.random.fold_in(key, 11)
    return draw_factor(key, 0.5, 5.0, 0.05)


def draw_right_stat(key, part):
    key = jax.random.fold_in(key, 17)
    return draw_factor(key, 0.5, 5.0, 0.05)


def draw_left_root(key, part):
    key = jax.random.fold_in(key, 23)
    return draw_factor(key, 0.3, 3.0, 0.6 * B ** (-0.5)).astype(jnp.bfloat16)


def draw_right_root(key, part):
    key = jax.random.fold_in(key, 29)
    return draw_factor(key, 0.3, 3.0, 0.6 * B ** (-0.5)).astype(jnp.bfloat16)


def block_scale(key, shape, cuts, least, top_value):
    loudness, own = 1.0, jax.random.fold_in(key, 6)
    for dim, parts in cuts:
        heights = jnp.exp(jax.random.uniform(jax.random.fold_in(own, dim), (parts,), jnp.float32, least / len(cuts), top_value / len(cuts)))
        loudness = loudness * jnp.repeat(heights, shape[dim] // parts).reshape([-1 if axis == dim else 1 for axis in range(len(shape))])
    return loudness


def deal_out(key, own, number, rows, amount, top, most, slope):
    order = jax.random.permutation(key, amount)
    heavy_load, usual = shares(amount, rows * top, most, slope, True), shares(amount, rows * top, most, slope, False)
    places = jnp.arange(amount)

    def named(sizes, offset_by):
        used = int((sizes > 0).sum())
        fixed = max(1, used // 4)
        moved = fixed + (places - fixed + offset_by * (used - fixed)) % max(1, amount - fixed)
        return jnp.zeros((amount,), jnp.int32).at[order[jnp.where(places < fixed, places, moved)]].set(jnp.asarray(sizes, jnp.int32))

    sizes = jnp.where(number % 4 == 0, named(heavy_load, number // 4), named(usual, number - number // 4 - 1))
    mixed = jax.random.permutation(jax.random.fold_in(own, 3), amount)
    source_of, receiver = mixed[0:amount // 2 * 2:2], mixed[1:amount // 2 * 2:2]
    margin = jnp.minimum(sizes[source_of] - 1, most - sizes[receiver]) // 2
    margin = jnp.where((source_of == order[0]) | (receiver == order[0]) | (sizes[receiver] == 0), 0, jnp.maximum(margin, 0))
    moved = jax.random.randint(jax.random.fold_in(own, 4), (amount // 2,), 0, 1 << 20) % (margin + 1)
    sizes = sizes.at[source_of].add(-moved).at[receiver].add(moved)
    labels = jnp.searchsorted(jnp.cumsum(sizes), jnp.arange(rows * top), side="right").astype(jnp.int32)
    grid = labels.reshape(top, rows).T
    grid = grid[jax.random.permutation(jax.random.fold_in(own, 1), rows)]
    offset_by = jax.random.randint(jax.random.fold_in(own, 2), (rows, 1), 0, top)
    return jnp.take_along_axis(grid, (jnp.arange(top)[None, :] + offset_by) % top, axis=1)


def shares(count, total, limit, skew, full):
    weights = [(1 << 20) // math.isqrt(grade ** skew) + 1 for grade in range(1, count + 1)]
    largest = limit if full else min(limit, max(-(-total // count), total * weights[0] // sum(weights)))
    least = 1 if total - largest >= count - 1 else 0
    given, surplus = [largest] + [least] * (count - 1), total - largest - least * (count - 1)
    while surplus > 0:
        candidates = [i for i in range(1, count) if given[i] < largest] or [i for i in range(1, count) if given[i] < limit]
        mass, left = sum([weights[i] for i in candidates]), surplus
        for i in candidates:
            addition = min(limit - given[i], max(1, left * weights[i] // mass), surplus)
            given[i] = given[i] + addition
            surplus = surplus - addition
    return np.array(given)


def setup_inputs(seed: int = 0) -> dict:
    seeds = jax.random.split(jax.random.key(seed), 8)
    partials = draw_partials(jax.random.fold_in(seeds[7], 71), 0)
    owners_keys = jax.random.split(jax.random.fold_in(seeds[1], 1), N_REPLICA * NBH // NBH)
    owners_turns = jax.random.permutation(jax.random.fold_in(seeds[1], 3), N_REPLICA * NBH // NBH)
    owners = jax.vmap(lambda own, number: deal_out(jax.random.fold_in(seeds[1], 2), own, number, NBH, N_FSDP, 1, SLOTS, 2))(owners_keys, owners_turns).reshape((N_REPLICA, NBH, 1))
    left_stat = draw_left_stat(jax.random.fold_in(seeds[7], 71), 0)
    right_stat = draw_right_stat(jax.random.fold_in(seeds[7], 71), 0)
    left_root = draw_left_root(jax.random.fold_in(seeds[7], 71), 0)
    right_root = draw_right_root(jax.random.fold_in(seeds[7], 71), 0)
    second_moment = jnp.clip(jnp.exp(math.log(3.0) - 3.4011974 * jax.random.uniform(seeds[6], (NS, B, B), jnp.float32) ** block_scale(seeds[6], (NS, B, B), ((0, 128),), -0.2, 0.2)), 0.1, 3.0)
    return dict(partials=partials, owners=owners, left_stat=left_stat, right_stat=right_stat, left_root=left_root, right_root=right_root, second_moment=second_moment)


FACTOR_DECAY = 0.9
MOMENT_DECAY = 0.99

def block_update(block_grad, left_old, right_old, root_left, root_right, moment_old):
    block_order = block_grad.shape[0]
    highest = lax.Precision.HIGHEST
    root_left = root_left.astype(jnp.float32)
    root_right = root_right.astype(jnp.float32)
    gram_left = jnp.dot(block_grad, block_grad.T, precision=highest, preferred_element_type=jnp.float32)
    gram_right = jnp.dot(block_grad.T, block_grad, precision=highest, preferred_element_type=jnp.float32)
    fresh_weight = (1.0 - FACTOR_DECAY) / block_order
    left_new = FACTOR_DECAY * left_old + fresh_weight * gram_left
    right_new = FACTOR_DECAY * right_old + fresh_weight * gram_right
    moment_new = MOMENT_DECAY * moment_old + (1.0 - MOMENT_DECAY) * block_grad * block_grad
    adam_step = block_grad / (jnp.sqrt(moment_new) + 1e-08)
    precond = jnp.dot(jnp.dot(root_left, block_grad, precision=highest, preferred_element_type=jnp.float32), root_right, precision=highest, preferred_element_type=jnp.float32)
    graft_scale = jnp.sqrt(jnp.mean(adam_step * adam_step)) / jnp.sqrt(jnp.mean(precond * precond) + 1e-06)
    update_block = (precond * graft_scale).astype(jnp.bfloat16)
    return (left_new, right_new, moment_new, update_block)

def slot_table(owners):
    owner_ids = owners[:, :, 0]
    position = jnp.arange(NBH, dtype=jnp.int32)
    same_owner = owner_ids[:, :, None] == owner_ids[:, None, :]
    earlier = position[None, None, :] < position[None, :, None]
    slot_rank = lax.optimization_barrier(jnp.sum((same_owner & earlier).astype(jnp.int32), axis=2))
    half_index = jnp.arange(N_REPLICA, dtype=jnp.int32)[:, None]
    return ((half_index * N_FSDP + owner_ids) * SLOTS + slot_rank).astype(jnp.int32).reshape(-1)

def reference(partials, owners, left_stat, right_stat, left_root, right_root, second_moment):
    gradient = lax.optimization_barrier(jnp.sum(partials.astype(jnp.float32), axis=0))
    target = slot_table(owners)

    def advance(index, state_carry):
        left_all, right_all, moment_all, update_all = state_carry
        slot_index = target[index]
        block_grad = lax.dynamic_slice_in_dim(gradient, index * B, B, 1)
        results = block_update(block_grad, lax.dynamic_index_in_dim(left_stat, slot_index, 0, keepdims=False), lax.dynamic_index_in_dim(right_stat, slot_index, 0, keepdims=False), lax.dynamic_index_in_dim(left_root, slot_index, 0, keepdims=False), lax.dynamic_index_in_dim(right_root, slot_index, 0, keepdims=False), lax.dynamic_index_in_dim(second_moment, slot_index, 0, keepdims=False))
        left_all = lax.dynamic_update_index_in_dim(left_all, results[0], slot_index, 0)
        right_all = lax.dynamic_update_index_in_dim(right_all, results[1], slot_index, 0)
        moment_all = lax.dynamic_update_index_in_dim(moment_all, results[2], slot_index, 0)
        update_all = lax.dynamic_update_slice_in_dim(update_all, results[3], index * B, 1)
        return (left_all, right_all, moment_all, update_all)
    start = (left_stat, right_stat, second_moment, jnp.zeros((B, C), jnp.bfloat16))
    left_next, right_next, moment_next, update = lax.fori_loop(0, NB, advance, start)
    return (left_next, right_next, moment_next, update)
```

```python
import jax
import jax.numpy as jnp
from jax import lax
from jax.experimental import pallas as pl
from jax.experimental.pallas import tpu as pltpu
from jax.sharding import PartitionSpec as P

FACTOR_DECAY = 0.9
MOMENT_DECAY = 0.99


def pack_kernel(source, half, mine, theirs, out):
    del half
    strip, order = 8, out.shape[1] // 3

    def summed(block):
        at = pl.ds(pl.multiple_of(block * order, order), order)
        return mine[:, at].astype(jnp.float32) + theirs[:, at].astype(jnp.float32)

    def step(i, carry):
        for q in range(3):
            pair = [summed(source[(2 * i + j) * 3 + q]) for j in range(2)]
            rows = pl.ds(pl.multiple_of(i * 2 * strip, 2 * strip), 2 * strip)
            out[rows, q * order : (q + 1) * order] = jnp.concatenate(pair, axis=0).astype(out.dtype)
        return carry

    lax.fori_loop(0, out.shape[0] // (2 * strip), step, 0, unroll=2)


def pack(source, half, partial, received, owners_count, slots, order):
    rows, columns = received.shape
    return pl.pallas_call(
        pack_kernel,
        grid_spec=pltpu.PrefetchScalarGridSpec(
            num_scalar_prefetch=2,
            grid=(1,),
            in_specs=[
                pl.BlockSpec((rows, columns), lambda i, source, half: (0, half[0])),
                pl.BlockSpec((rows, columns), lambda i, source, half: (0, 0)),
            ],
            out_specs=pl.BlockSpec((owners_count * rows, slots * order), lambda i, source, half: (0, 0)),
        ),
        out_shape=jax.ShapeDtypeStruct((owners_count * rows, slots * order), jnp.bfloat16),
        compiler_params=pltpu.CompilerParams(vmem_limit_bytes=24 * 2**20),
    )(source, half, partial, received)


def update_kernel(grad, root_left, root_right, moment, out):
    g = grad[...]
    count = float(g.shape[0] * g.shape[1])
    left = jnp.dot(root_left[0], g, preferred_element_type=jnp.float32)
    high = left.astype(jnp.bfloat16)
    low = (left - high.astype(jnp.float32)).astype(jnp.bfloat16)
    right = root_right[0]
    shampoo = jnp.dot(high, right, preferred_element_type=jnp.float32) + jnp.dot(
        low, right, preferred_element_type=jnp.float32
    )
    g = g.astype(jnp.float32)
    fresh = MOMENT_DECAY * moment[0] + (1.0 - MOMENT_DECAY) * g * g
    adam = g / (jnp.sqrt(fresh) + 1e-08)
    scale = jnp.sqrt(jnp.sum(adam * adam) / count) / jnp.sqrt(
        jnp.sum(shampoo * shampoo) / count + 1e-06
    )
    out[...] = (shampoo * scale).astype(out.dtype)


def updates(grads, root_left, root_right, moment):
    slots, order, _ = moment.shape
    slot = pl.BlockSpec((1, order, order), lambda s: (s, 0, 0))
    columns = pl.BlockSpec((order, order), lambda s: (0, s))
    return pl.pallas_call(
        update_kernel,
        grid=(slots,),
        in_specs=[columns, slot, slot, slot],
        out_specs=columns,
        out_shape=jax.ShapeDtypeStruct(grads.shape, jnp.bfloat16),
        compiler_params=pltpu.CompilerParams(vmem_limit_bytes=32 * 2**20),
    )(grads, root_left, root_right, moment)


def state_kernel(load, grad, left, right, moment, left_out, right_out, moment_out):
    active = pl.program_id(0) < load[0]

    @pl.when(active)
    def _():
        g = grad[...]
        weight = (1.0 - FACTOR_DECAY) / g.shape[0]
        gram = lax.dot_general(g, g, (((1,), (1,)), ((), ())), preferred_element_type=jnp.float32)
        left_out[0] = FACTOR_DECAY * left[0] + weight * gram
        gram = lax.dot_general(g, g, (((0,), (0,)), ((), ())), preferred_element_type=jnp.float32)
        right_out[0] = FACTOR_DECAY * right[0] + weight * gram
        g = g.astype(jnp.float32)
        moment_out[0] = MOMENT_DECAY * moment[0] + (1.0 - MOMENT_DECAY) * g * g

    @pl.when(jnp.logical_not(active))
    def _():
        left_out[...] = left[...]
        right_out[...] = right[...]
        moment_out[...] = moment[...]


def states(load, grads, left, right, moment):
    slots, order, _ = moment.shape
    slot = pl.BlockSpec((1, order, order), lambda s, load: (s, 0, 0))
    columns = pl.BlockSpec((order, order), lambda s, load: (0, s))
    kept = jax.ShapeDtypeStruct(moment.shape, jnp.float32)
    return pl.pallas_call(
        state_kernel,
        grid_spec=pltpu.PrefetchScalarGridSpec(
            num_scalar_prefetch=1,
            grid=(slots,),
            in_specs=[columns, slot, slot, slot],
            out_specs=[slot, slot, slot],
        ),
        out_shape=[kept, kept, kept],
        compiler_params=pltpu.CompilerParams(vmem_limit_bytes=32 * 2**20),
        cost_estimate=pl.CostEstimate(
            flops=4 * slots * order**3, bytes_accessed=26 * slots * order**2, transcendentals=0
        ),
    )(load, grads, left, right, moment)


def unpack_kernel(owner, rank, arrived, out):
    strip, order = out.shape[0], arrived.shape[1] // 3
    blocks = out.shape[1] // order
    first = pl.program_id(0) * blocks

    def step(k, carry):
        o, q = owner[first + k], rank[first + k]
        rows = pl.ds(pl.multiple_of(o // 2 * (2 * strip), 2 * strip), 2 * strip)
        at = pl.ds(pl.multiple_of(q * order, order), order)
        both = arrived[rows, at].astype(jnp.float32)
        piece = jnp.where(o % 2 == 0, both[:strip], both[strip:])
        out[:, pl.ds(pl.multiple_of(k * order, order), order)] = piece.astype(out.dtype)
        return carry

    lax.fori_loop(0, blocks, step, 0, unroll=4)


def unpack(owner, rank, arrived, strip, order):
    columns = owner.shape[0] * order
    steps = 4
    return pl.pallas_call(
        unpack_kernel,
        grid_spec=pltpu.PrefetchScalarGridSpec(
            num_scalar_prefetch=2,
            grid=(steps,),
            in_specs=[pl.BlockSpec(arrived.shape, lambda i, owner, rank: (0, 0))],
            out_specs=pl.BlockSpec((strip, columns // steps), lambda i, owner, rank: (0, i)),
        ),
        out_shape=jax.ShapeDtypeStruct((strip, columns), jnp.bfloat16),
        compiler_params=pltpu.CompilerParams(vmem_limit_bytes=24 * 2**20),
    )(owner, rank, arrived)


def shards(partials, owners, left_stat, right_stat, left_root, right_root, second_moment):
    fsdp_count = lax.axis_size("fsdp")
    slots, order, _ = left_stat.shape
    strip = partials.shape[1]
    half_blocks = owners.shape[1]
    my_half = lax.axis_index("replica")
    my_fsdp = lax.axis_index("fsdp")
    partial = partials[0]
    half_columns = half_blocks * order
    leaving = lax.dynamic_slice_in_dim(partial, (1 - my_half) * half_columns, half_columns, 1)
    received = lax.ppermute(leaving, "replica", [(0, 1), (1, 0)])

    owner = lax.dynamic_index_in_dim(owners[:, :, 0], my_half, 0, keepdims=False)
    position = jnp.arange(half_blocks, dtype=jnp.int32)
    same = owner[:, None] == owner[None, :]
    rank = jnp.sum((same & (position[None, :] < position[:, None])).astype(jnp.int32), axis=1)
    target = owner * slots + rank
    places = jnp.arange(fsdp_count * slots, dtype=jnp.int32)
    source = jnp.sum(jnp.where(target[None, :] == places[:, None], position[None, :], 0), axis=1)
    load = jnp.sum((owner == my_fsdp).astype(jnp.int32)).reshape(1)

    outgoing = pack(source, my_half.astype(jnp.int32).reshape(1), partial, received, fsdp_count, slots, order)
    grads = lax.all_to_all(outgoing, "fsdp", split_axis=0, concat_axis=0, tiled=True)
    fresh = updates(grads, left_root, right_root, second_moment)
    arrived = lax.all_to_all(fresh, "fsdp", split_axis=0, concat_axis=0, tiled=True)
    left_next, right_next, moment_next = states(load, grads, left_stat, right_stat, second_moment)
    update = unpack(owner, rank, arrived, strip, order)
    return (left_next, right_next, moment_next, update)


def solution(mesh):
    placed = (
        P("replica", "fsdp", None),
        P(),
        P(("replica", "fsdp"), None, None),
        P(("replica", "fsdp"), None, None),
        P(("replica", "fsdp"), None, None),
        P(("replica", "fsdp"), None, None),
        P(("replica", "fsdp"), None, None),
    )
    return jax.shard_map(
        shards,
        mesh=mesh,
        in_specs=placed,
        out_specs=(
            P(("replica", "fsdp"), None, None),
            P(("replica", "fsdp"), None, None),
            P(("replica", "fsdp"), None, None),
            P("fsdp", "replica"),
        ),
        check_vma=False,
    )
```

```python
import jax
import jax.numpy as jnp
from jax import lax
from jax.experimental import pallas as pl
from jax.experimental.pallas import tpu as pltpu
from jax.sharding import PartitionSpec as P

FACTOR_DECAY = 0.9
MOMENT_DECAY = 0.99


def pack_kernel(source, half, mine, theirs, out):
    strip, order = 8, out.shape[1] // 3
    first = half[0] * mine.shape[1]

    def summed(block):
        at = pl.ds(pl.multiple_of(block * order, order), order)
        same = pl.ds(pl.multiple_of(first + block * order, order), order)
        return mine[:, at].astype(jnp.float32) + theirs[:, same].astype(jnp.float32)

    def step(i, carry):
        for q in range(3):
            pair = [summed(source[(2 * i + j) * 3 + q]) for j in range(2)]
            rows = pl.ds(pl.multiple_of(i * 2 * strip, 2 * strip), 2 * strip)
            out[rows, q * order : (q + 1) * order] = jnp.concatenate(pair, axis=0).astype(out.dtype)
        return carry

    lax.fori_loop(0, out.shape[0] // (2 * strip), step, 0, unroll=4)


def pack(source, half, mine, theirs, destinations, slots, order):
    few, near = pl.BlockSpec(memory_space=pltpu.SMEM), pl.BlockSpec(memory_space=pltpu.VMEM)
    return pl.pallas_call(
        pack_kernel,
        in_specs=[few, few, near, near],
        out_specs=near,
        out_shape=jax.ShapeDtypeStruct((destinations * mine.shape[0], slots * order), jnp.bfloat16),
        compiler_params=pltpu.CompilerParams(vmem_limit_bytes=16 * 2**20),
    )(source, half, mine, theirs)


def update_kernel(grads, root_left, root_right, moment, out, half_way, shampoo, result, sent):
    slots, order, _ = moment.shape
    chunk, count = 64, float(order * order)

    def folded(square):
        return jnp.sum(square.reshape(-1, 8, order), axis=0)

    copies = []
    for s in range(slots):
        columns = slice(s * order, (s + 1) * order)
        left = jnp.dot(root_left[s], grads[:, columns], preferred_element_type=jnp.float32)
        half_way[s] = left.astype(half_way.dtype)
        shampoo[s] = jnp.dot(half_way[s], root_right[s], preferred_element_type=jnp.float32)
        adam_square = jnp.zeros((8, order), jnp.float32)
        shampoo_square = jnp.zeros((8, order), jnp.float32)
        for i in range(0, order, chunk):
            rows = slice(i, i + chunk)
            g = grads[rows, columns].astype(jnp.float32)
            fresh = MOMENT_DECAY * moment[s, rows] + (1.0 - MOMENT_DECAY) * g * g
            adam = g / (fresh * lax.rsqrt(fresh) + 1e-08)
            adam_square = adam_square + folded(adam * adam)
            shampoo_square = shampoo_square + folded(shampoo[s, rows] * shampoo[s, rows])
        scale = jnp.sqrt(jnp.sum(adam_square) / count) / jnp.sqrt(
            jnp.sum(shampoo_square) / count + 1e-06
        )
        for i in range(0, order, chunk):
            rows = slice(i, i + chunk)
            result[s, rows] = (shampoo[s, rows] * scale).astype(result.dtype)
        copies.append(pltpu.make_async_copy(result.at[s], out.at[:, columns], sent.at[s]))
        copies[s].start()
    for copy in copies:
        copy.wait()


def updates(grads, root_left, root_right, moment):
    slots, order, _ = moment.shape
    near = pl.BlockSpec(memory_space=pltpu.VMEM)
    return pl.pallas_call(
        update_kernel,
        in_specs=[near] * 4,
        out_specs=pl.BlockSpec(memory_space=pltpu.HBM),
        out_shape=pltpu.HBM(grads.shape, jnp.bfloat16),
        scratch_shapes=[
            pltpu.VMEM((slots, order, order), jnp.bfloat16),
            pltpu.VMEM((slots, order, order), jnp.float32),
            pltpu.VMEM((slots, order, order), jnp.bfloat16),
            pltpu.SemaphoreType.DMA((slots,)),
        ],
        compiler_params=pltpu.CompilerParams(vmem_limit_bytes=24 * 2**20),
    )(grads, root_left, root_right, moment)


def state_kernel(load, grad, left, right, moment, left_out, right_out, moment_out):
    active = pl.program_id(0) < load[0]

    @pl.when(active)
    def _():
        g = grad[...]
        weight = (1.0 - FACTOR_DECAY) / g.shape[0]
        gram = lax.dot_general(g, g, (((1,), (1,)), ((), ())), preferred_element_type=jnp.float32)
        left_out[0] = FACTOR_DECAY * left[0] + weight * gram
        gram = lax.dot_general(g, g, (((0,), (0,)), ((), ())), preferred_element_type=jnp.float32)
        right_out[0] = FACTOR_DECAY * right[0] + weight * gram
        g = g.astype(jnp.float32)
        moment_out[0] = MOMENT_DECAY * moment[0] + (1.0 - MOMENT_DECAY) * g * g

    @pl.when(jnp.logical_not(active))
    def _():
        left_out[...] = left[...]
        right_out[...] = right[...]
        moment_out[...] = moment[...]


def states(load, grads, left, right, moment):
    slots, order, _ = moment.shape
    slot = pl.BlockSpec((1, order, order), lambda s, load: (s, 0, 0))
    columns = pl.BlockSpec((order, order), lambda s, load: (0, s))
    kept = jax.ShapeDtypeStruct(moment.shape, jnp.float32)
    return pl.pallas_call(
        state_kernel,
        grid_spec=pltpu.PrefetchScalarGridSpec(
            num_scalar_prefetch=1,
            grid=(slots,),
            in_specs=[columns, slot, slot, slot],
            out_specs=[slot, slot, slot],
        ),
        out_shape=[kept, kept, kept],
        compiler_params=pltpu.CompilerParams(vmem_limit_bytes=32 * 2**20),
        cost_estimate=pl.CostEstimate(
            flops=4 * slots * order**3, bytes_accessed=26 * slots * order**2, transcendentals=0
        ),
    )(load, grads, left, right, moment)


def unpack_kernel(owner, rank, arrived, out, rows, sent):
    order = arrived.shape[2] // 3
    blocks, copies = owner.shape[0], sent.shape[0]
    each = blocks // copies
    started = []
    for c in range(copies):

        def step(i, carry):
            k = c * each + i
            at = pl.ds(pl.multiple_of(rank[k] * order, order), order)
            to = pl.ds(pl.multiple_of(k * order, order), order)
            rows[:, to] = arrived[owner[k], :, at]
            return carry

        lax.fori_loop(0, each, step, 0, unroll=True)
        part = pl.ds(c * each * order, each * order)
        started.append(pltpu.make_async_copy(rows.at[:, part], out.at[:, part], sent.at[c]))
        started[c].start()
    for copy in started:
        copy.wait()


def unpack(owner, rank, arrived):
    _, strip, width = arrived.shape
    columns = owner.shape[0] * (width // 3)
    few = pl.BlockSpec(memory_space=pltpu.SMEM)
    return pl.pallas_call(
        unpack_kernel,
        in_specs=[few, few, pl.BlockSpec(memory_space=pltpu.VMEM)],
        out_specs=pl.BlockSpec(memory_space=pltpu.HBM),
        out_shape=jax.ShapeDtypeStruct((strip, columns), jnp.bfloat16),
        scratch_shapes=[pltpu.VMEM((strip, columns), jnp.bfloat16), pltpu.SemaphoreType.DMA((4,))],
        compiler_params=pltpu.CompilerParams(vmem_limit_bytes=16 * 2**20),
    )(owner, rank, arrived)


def half_kernel(which, partial, out, copied):
    columns = out.shape[1]
    at = pl.ds(pl.multiple_of(which[0] * columns, columns), columns)
    copy = pltpu.make_async_copy(partial.at[:, at], out, copied)
    copy.start()
    copy.wait()


def half_columns(which, partial):
    rows, columns = partial.shape
    return pl.pallas_call(
        half_kernel,
        in_specs=[pl.BlockSpec(memory_space=pltpu.SMEM), pl.BlockSpec(memory_space=pltpu.HBM)],
        out_specs=pl.BlockSpec(memory_space=pltpu.VMEM),
        out_shape=pltpu.VMEM((rows, columns // 2), partial.dtype),
        scratch_shapes=[pltpu.SemaphoreType.DMA],
        compiler_params=pltpu.CompilerParams(vmem_limit_bytes=8 * 2**20),
    )(which, pltpu.with_memory_space_constraint(partial, pltpu.HBM))


def shards(partials, owners, left_stat, right_stat, left_root, right_root, second_moment):
    fsdp_count = lax.axis_size("fsdp")
    slots, order, _ = left_stat.shape
    strip = partials.shape[1]
    half_blocks = owners.shape[1]
    my_half = lax.axis_index("replica")
    my_fsdp = lax.axis_index("fsdp")
    partial = partials[0]
    half = my_half.astype(jnp.int32).reshape(1)
    mine = half_columns(half, partial)
    received = lax.ppermute(partial, "replica", [(0, 1), (1, 0)])

    owner = lax.dynamic_index_in_dim(owners[:, :, 0], my_half, 0, keepdims=False)
    position = jnp.arange(half_blocks, dtype=jnp.int32)
    same = owner[:, None] == owner[None, :]
    rank = jnp.sum((same & (position[None, :] < position[:, None])).astype(jnp.int32), axis=1)
    target = owner * slots + rank
    places = jnp.arange(fsdp_count * slots, dtype=jnp.int32)
    source = jnp.sum(jnp.where(target[None, :] == places[:, None], position[None, :], 0), axis=1)
    load = jnp.sum((owner == my_fsdp).astype(jnp.int32)).reshape(1)

    outgoing = pack(source, half, mine, received, fsdp_count, slots, order)
    grads = lax.all_to_all(outgoing, "fsdp", split_axis=0, concat_axis=0, tiled=True)
    fresh = updates(grads, left_root, right_root, second_moment)
    arrived = lax.all_to_all(fresh, "fsdp", split_axis=0, concat_axis=0, tiled=True)
    left_next, right_next, moment_next = states(load, grads, left_stat, right_stat, second_moment)
    update = unpack(owner, rank, arrived.reshape(fsdp_count, strip, slots * order))
    return (left_next, right_next, moment_next, update)


def solution(mesh):
    placed = (
        P("replica", "fsdp", None),
        P(),
        P(("replica", "fsdp"), None, None),
        P(("replica", "fsdp"), None, None),
        P(("replica", "fsdp"), None, None),
        P(("replica", "fsdp"), None, None),
        P(("replica", "fsdp"), None, None),
    )
    return jax.shard_map(
        shards,
        mesh=mesh,
        in_specs=placed,
        out_specs=(
            P(("replica", "fsdp"), None, None),
            P(("replica", "fsdp"), None, None),
            P(("replica", "fsdp"), None, None),
            P("fsdp", "replica"),
        ),
        check_vma=False,
    )
```

```python
import jax
import jax.numpy as jnp
from jax import lax
from jax.experimental import pallas as pl
from jax.experimental.pallas import tpu as pltpu
from jax.sharding import PartitionSpec as P

FACTOR_DECAY = 0.9
MOMENT_DECAY = 0.99


def pack_kernel(source, mine, theirs, out):
    strip, order = 8, out.shape[1] // 3

    def summed(block):
        at = pl.ds(pl.multiple_of(block * order, order), order)
        return mine[:, at].astype(jnp.float32) + theirs[:, at].astype(jnp.float32)

    def step(i, carry):
        for q in range(3):
            pair = [summed(source[(2 * i + j) * 3 + q]) for j in range(2)]
            rows = pl.ds(pl.multiple_of(i * 2 * strip, 2 * strip), 2 * strip)
            out[rows, q * order : (q + 1) * order] = jnp.concatenate(pair, axis=0).astype(out.dtype)
        return carry

    lax.fori_loop(0, out.shape[0] // (2 * strip), step, 0, unroll=4)


def pack(source, mine, theirs, destinations, slots, order):
    few, near = pl.BlockSpec(memory_space=pltpu.SMEM), pl.BlockSpec(memory_space=pltpu.VMEM)
    return pl.pallas_call(
        pack_kernel,
        in_specs=[few, near, near],
        out_specs=near,
        out_shape=jax.ShapeDtypeStruct((destinations * mine.shape[0], slots * order), jnp.bfloat16),
        compiler_params=pltpu.CompilerParams(vmem_limit_bytes=16 * 2**20),
    )(source, mine, theirs)


def update_kernel(grads, root_left, root_right, moment, out, half_way, shampoo, result, sent):
    slots, order, _ = moment.shape
    chunk, parts, count = 64, sent.shape[1], float(order * order)

    def folded(square):
        return jnp.sum(square.reshape(-1, 8, order), axis=0)

    def columns(s):
        return slice(s * order, (s + 1) * order)

    def first(s, rows):
        left = jnp.dot(root_left[s, rows], grads[:, columns(s)], preferred_element_type=jnp.float32)
        half_way[s, rows] = left.astype(half_way.dtype)

    def second(s, rows):
        both = jnp.dot(half_way[s, rows], root_right[s], preferred_element_type=jnp.float32)
        shampoo[s, rows] = both
        return folded(both * both)

    def adam(s, part):
        total = jnp.zeros((8, order), jnp.float32)
        for i in range(part * order // 4, (part + 1) * order // 4, chunk):
            rows = slice(i, i + chunk)
            g = grads[rows, columns(s)].astype(jnp.float32)
            fresh = MOMENT_DECAY * moment[s, rows] + (1.0 - MOMENT_DECAY) * g * g
            step = g / (fresh * lax.rsqrt(fresh) + 1e-08)
            total = total + folded(step * step)
        return total

    upper, lower = slice(0, order // 2), slice(order // 2, order)
    copies = []
    for s in range(slots):
        first(s, upper)
        adam_square = adam(s, 0)
        first(s, lower)
        adam_square = adam_square + adam(s, 1)
        shampoo_square = second(s, upper)
        adam_square = adam_square + adam(s, 2)
        shampoo_square = shampoo_square + second(s, lower)
        adam_square = adam_square + adam(s, 3)
        scale = jnp.sqrt(jnp.sum(adam_square) / count) / jnp.sqrt(
            jnp.sum(shampoo_square) / count + 1e-06
        )
        for p in range(parts):
            rows = slice(p * order // parts, (p + 1) * order // parts)
            result[s, rows] = (shampoo[s, rows] * scale).astype(result.dtype)
            copies.append(
                pltpu.make_async_copy(result.at[s, rows], out.at[rows, columns(s)], sent.at[s, p])
            )
            copies[-1].start()
    for copy in copies:
        copy.wait()


def updates(grads, root_left, root_right, moment):
    slots, order, _ = moment.shape
    near = pl.BlockSpec(memory_space=pltpu.VMEM)
    return pl.pallas_call(
        update_kernel,
        in_specs=[near] * 4,
        out_specs=pl.BlockSpec(memory_space=pltpu.HBM),
        out_shape=pltpu.HBM(grads.shape, jnp.bfloat16),
        scratch_shapes=[
            pltpu.VMEM((slots, order, order), jnp.bfloat16),
            pltpu.VMEM((slots, order, order), jnp.float32),
            pltpu.VMEM((slots, order, order), jnp.bfloat16),
            pltpu.SemaphoreType.DMA((slots, 2)),
        ],
        compiler_params=pltpu.CompilerParams(vmem_limit_bytes=24 * 2**20),
    )(grads, root_left, root_right, moment)


def state_kernel(load, grad, left, right, moment, left_out, right_out, moment_out):
    active = pl.program_id(0) < load[0]

    @pl.when(active)
    def _():
        g = grad[...]
        weight = (1.0 - FACTOR_DECAY) / g.shape[0]
        gram = lax.dot_general(g, g, (((1,), (1,)), ((), ())), preferred_element_type=jnp.float32)
        left_out[0] = FACTOR_DECAY * left[0] + weight * gram
        gram = lax.dot_general(g, g, (((0,), (0,)), ((), ())), preferred_element_type=jnp.float32)
        right_out[0] = FACTOR_DECAY * right[0] + weight * gram
        g = g.astype(jnp.float32)
        moment_out[0] = MOMENT_DECAY * moment[0] + (1.0 - MOMENT_DECAY) * g * g

    @pl.when(jnp.logical_not(active))
    def _():
        left_out[...] = left[...]
        right_out[...] = right[...]
        moment_out[...] = moment[...]


def states(load, grads, left, right, moment):
    slots, order, _ = moment.shape
    slot = pl.BlockSpec((1, order, order), lambda s, load: (s, 0, 0))
    columns = pl.BlockSpec((order, order), lambda s, load: (0, s))
    kept = jax.ShapeDtypeStruct(moment.shape, jnp.float32)
    return pl.pallas_call(
        state_kernel,
        grid_spec=pltpu.PrefetchScalarGridSpec(
            num_scalar_prefetch=1,
            grid=(slots,),
            in_specs=[columns, slot, slot, slot],
            out_specs=[slot, slot, slot],
        ),
        out_shape=[kept, kept, kept],
        compiler_params=pltpu.CompilerParams(vmem_limit_bytes=32 * 2**20),
        cost_estimate=pl.CostEstimate(
            flops=4 * slots * order**3, bytes_accessed=26 * slots * order**2, transcendentals=0
        ),
    )(load, grads, left, right, moment)


def unpack_kernel(owner, rank, arrived, out, rows, sent):
    order = arrived.shape[2] // 3
    blocks, copies = owner.shape[0], sent.shape[0]
    each = blocks // copies
    started = []
    for c in range(copies):

        def step(i, carry):
            k = c * each + i
            at = pl.ds(pl.multiple_of(rank[k] * order, order), order)
            to = pl.ds(pl.multiple_of(k * order, order), order)
            rows[:, to] = arrived[owner[k], :, at]
            return carry

        lax.fori_loop(0, each, step, 0, unroll=True)
        part = pl.ds(c * each * order, each * order)
        started.append(pltpu.make_async_copy(rows.at[:, part], out.at[:, part], sent.at[c]))
        started[c].start()
    for copy in started:
        copy.wait()


def unpack(owner, rank, arrived):
    _, strip, width = arrived.shape
    columns = owner.shape[0] * (width // 3)
    few = pl.BlockSpec(memory_space=pltpu.SMEM)
    return pl.pallas_call(
        unpack_kernel,
        in_specs=[few, few, pl.BlockSpec(memory_space=pltpu.VMEM)],
        out_specs=pl.BlockSpec(memory_space=pltpu.HBM),
        out_shape=jax.ShapeDtypeStruct((strip, columns), jnp.bfloat16),
        scratch_shapes=[pltpu.VMEM((strip, columns), jnp.bfloat16), pltpu.SemaphoreType.DMA((4,))],
        compiler_params=pltpu.CompilerParams(vmem_limit_bytes=16 * 2**20),
    )(owner, rank, arrived)


def half_kernel(which, partial, out, copied):
    pieces = copied.shape[0]
    columns = out.shape[1] // pieces
    copies = []
    for i in range(pieces):
        at = pl.ds(pl.multiple_of((which[0] * pieces + i) * columns, columns), columns)
        copies.append(
            pltpu.make_async_copy(
                partial.at[:, at], out.at[:, i * columns : (i + 1) * columns], copied.at[i]
            )
        )
        copies[i].start()
    for copy in copies:
        copy.wait()


def half_columns(which, partial):
    rows, columns = partial.shape
    return pl.pallas_call(
        half_kernel,
        in_specs=[pl.BlockSpec(memory_space=pltpu.SMEM), pl.BlockSpec(memory_space=pltpu.HBM)],
        out_specs=pl.BlockSpec(memory_space=pltpu.VMEM),
        out_shape=pltpu.VMEM((rows, columns // 2), partial.dtype),
        scratch_shapes=[pltpu.SemaphoreType.DMA((4,))],
        compiler_params=pltpu.CompilerParams(vmem_limit_bytes=8 * 2**20),
    )(which, pltpu.with_memory_space_constraint(partial, pltpu.HBM))


def shards(partials, owners, left_stat, right_stat, left_root, right_root, second_moment):
    fsdp_count = lax.axis_size("fsdp")
    slots, order, _ = left_stat.shape
    strip = partials.shape[1]
    half_blocks = owners.shape[1]
    my_half = lax.axis_index("replica")
    my_fsdp = lax.axis_index("fsdp")
    partial = partials[0]
    half = my_half.astype(jnp.int32).reshape(1)
    received = lax.ppermute(half_columns(1 - half, partial), "replica", [(0, 1), (1, 0)])
    mine = half_columns(half, partial)

    owner = lax.dynamic_index_in_dim(owners[:, :, 0], my_half, 0, keepdims=False)
    position = jnp.arange(half_blocks, dtype=jnp.int32)
    same = owner[:, None] == owner[None, :]
    rank = jnp.sum((same & (position[None, :] < position[:, None])).astype(jnp.int32), axis=1)
    target = owner * slots + rank
    places = jnp.arange(fsdp_count * slots, dtype=jnp.int32)
    source = jnp.sum(jnp.where(target[None, :] == places[:, None], position[None, :], 0), axis=1)
    load = jnp.sum((owner == my_fsdp).astype(jnp.int32)).reshape(1)

    outgoing = pack(source, mine, received, fsdp_count, slots, order)
    grads = lax.all_to_all(outgoing, "fsdp", split_axis=0, concat_axis=0, tiled=True)
    fresh = updates(grads, left_root, right_root, second_moment)
    arrived = lax.all_to_all(fresh, "fsdp", split_axis=0, concat_axis=0, tiled=True)
    left_next, right_next, moment_next = states(load, grads, left_stat, right_stat, second_moment)
    update = unpack(owner, rank, arrived.reshape(fsdp_count, strip, slots * order))
    return (left_next, right_next, moment_next, update)


def solution(mesh):
    placed = (
        P("replica", "fsdp", None),
        P(),
        P(("replica", "fsdp"), None, None),
        P(("replica", "fsdp"), None, None),
        P(("replica", "fsdp"), None, None),
        P(("replica", "fsdp"), None, None),
        P(("replica", "fsdp"), None, None),
    )
    return jax.shard_map(
        shards,
        mesh=mesh,
        in_specs=placed,
        out_specs=(
            P(("replica", "fsdp"), None, None),
            P(("replica", "fsdp"), None, None),
            P(("replica", "fsdp"), None, None),
            P("fsdp", "replica"),
        ),
        check_vma=False,
    )
```

```python
import functools

import jax
import jax.numpy as jnp
from jax import lax
from jax.experimental import pallas as pl
from jax.experimental.pallas import tpu as pltpu
from jax.sharding import PartitionSpec as P

FACTOR_DECAY = 0.9
MOMENT_DECAY = 0.99


def pack_kernel(source, mine, theirs, out):
    strip, order = 8, out.shape[1] // 3

    def summed(block):
        at = pl.ds(pl.multiple_of(block * order, order), order)
        return mine[:, at].astype(jnp.float32) + theirs[:, at].astype(jnp.float32)

    def step(i, carry):
        for q in range(3):
            pair = [summed(source[0, (2 * i + j) * 3 + q]) for j in range(2)]
            rows = pl.ds(pl.multiple_of(i * 2 * strip, 2 * strip), 2 * strip)
            out[rows, q * order : (q + 1) * order] = jnp.concatenate(pair, axis=0).astype(out.dtype)
        return carry

    lax.fori_loop(0, out.shape[0] // (2 * strip), step, 0, unroll=4)


def pack(source, mine, theirs, destinations, slots, order):
    few, near = pl.BlockSpec(memory_space=pltpu.SMEM), pl.BlockSpec(memory_space=pltpu.VMEM)
    return pl.pallas_call(
        pack_kernel,
        in_specs=[few, near, near],
        out_specs=near,
        out_shape=jax.ShapeDtypeStruct((destinations * mine.shape[0], slots * order), jnp.bfloat16),
        compiler_params=pltpu.CompilerParams(vmem_limit_bytes=16 * 2**20),
    )(source, mine, theirs)


def update_kernel(grads, root_left, root_right, moment, out, half_way, shampoo, result, sent):
    slots, order, _ = moment.shape
    parts, count = sent.shape[1], float(order * order)

    def folded(square):
        return jnp.sum(square.reshape(-1, 8, order), axis=0)

    def columns(s):
        return slice(s * order, (s + 1) * order)

    def rows_of(part, of=parts):
        return slice(part * order // of, (part + 1) * order // of)

    zero = jnp.zeros((8, order), jnp.float32)
    adam_square = [zero] * slots
    chunks = [(s, i) for s in range(slots) for i in range(16)]
    each = len(chunks) // (slots * parts)
    for step in range(slots * parts):
        s, rows = step // parts, rows_of(step % parts)
        left = jnp.dot(root_left[s, rows], grads[:, columns(s)], preferred_element_type=jnp.float32)
        half_way[s, rows] = left.astype(half_way.dtype)
        for r, i in chunks[step * each : (step + 1) * each]:
            some = rows_of(i, 16)
            g = grads[some, columns(r)].astype(jnp.float32)
            fresh = MOMENT_DECAY * moment[r, some] + (1.0 - MOMENT_DECAY) * g * g
            adam = g / (fresh * lax.rsqrt(fresh) + 1e-08)
            adam_square[r] = adam_square[r] + folded(adam * adam)
    copies = []
    for s in range(slots):
        shampoo_square = zero
        for part in range(parts):
            rows = rows_of(part)
            both = jnp.dot(half_way[s, rows], root_right[s], preferred_element_type=jnp.float32)
            shampoo[s, rows] = both
            shampoo_square = shampoo_square + folded(both * both)
        scale = jnp.sqrt(jnp.sum(adam_square[s]) / count) / jnp.sqrt(
            jnp.sum(shampoo_square) / count + 1e-06
        )
        for part in range(parts):
            rows = rows_of(part)
            result[s, rows] = (shampoo[s, rows] * scale).astype(result.dtype)
            copies.append(
                pltpu.make_async_copy(
                    result.at[s, rows], out.at[rows, columns(s)], sent.at[s, part]
                )
            )
            copies[-1].start()
    for copy in copies:
        copy.wait()


def updates(grads, root_left, root_right, moment):
    slots, order, _ = moment.shape
    near = pl.BlockSpec(memory_space=pltpu.VMEM)
    return pl.pallas_call(
        update_kernel,
        in_specs=[near] * 4,
        out_specs=pl.BlockSpec(memory_space=pltpu.HBM),
        out_shape=pltpu.HBM(grads.shape, jnp.bfloat16),
        scratch_shapes=[
            pltpu.VMEM((slots, order, order), jnp.bfloat16),
            pltpu.VMEM((slots, order, order), jnp.float32),
            pltpu.VMEM((slots, order, order), jnp.bfloat16),
            pltpu.SemaphoreType.DMA((slots, 4)),
        ],
        compiler_params=pltpu.CompilerParams(vmem_limit_bytes=24 * 2**20),
    )(grads, root_left, root_right, moment)


def state_kernel(load, grad, left, right, moment, left_out, right_out, moment_out):
    active = pl.program_id(0) < load[0, 0]

    @pl.when(active)
    def _():
        g = grad[...]
        weight = (1.0 - FACTOR_DECAY) / g.shape[0]
        gram = lax.dot_general(g, g, (((1,), (1,)), ((), ())), preferred_element_type=jnp.float32)
        left_out[0] = FACTOR_DECAY * left[0] + weight * gram
        gram = lax.dot_general(g, g, (((0,), (0,)), ((), ())), preferred_element_type=jnp.float32)
        right_out[0] = FACTOR_DECAY * right[0] + weight * gram
        g = g.astype(jnp.float32)
        moment_out[0] = MOMENT_DECAY * moment[0] + (1.0 - MOMENT_DECAY) * g * g

    @pl.when(jnp.logical_not(active))
    def _():
        left_out[...] = left[...]
        right_out[...] = right[...]
        moment_out[...] = moment[...]


def states(load, grads, left, right, moment):
    slots, order, _ = moment.shape
    slot = pl.BlockSpec((1, order, order), lambda s, load: (s, 0, 0))
    columns = pl.BlockSpec((order, order), lambda s, load: (0, s))
    kept = jax.ShapeDtypeStruct(moment.shape, jnp.float32)
    return pl.pallas_call(
        state_kernel,
        grid_spec=pltpu.PrefetchScalarGridSpec(
            num_scalar_prefetch=1,
            grid=(slots,),
            in_specs=[columns, slot, slot, slot],
            out_specs=[slot, slot, slot],
        ),
        out_shape=[kept, kept, kept],
        compiler_params=pltpu.CompilerParams(vmem_limit_bytes=32 * 2**20),
        cost_estimate=pl.CostEstimate(
            flops=4 * slots * order**3, bytes_accessed=26 * slots * order**2, transcendentals=0
        ),
    )(load, grads, left, right, moment)


def unpack_kernel(place, arrived, out, rows, sent):
    order = arrived.shape[2] // 3
    blocks, copies = place.shape[1], sent.shape[0]
    each = blocks // copies
    started = []
    for c in range(copies):

        def step(i, carry):
            k = c * each + i
            at = pl.ds(pl.multiple_of(place[1, k] * order, order), order)
            to = pl.ds(pl.multiple_of(k * order, order), order)
            rows[:, to] = arrived[place[0, k], :, at]
            return carry

        lax.fori_loop(0, each, step, 0, unroll=True)
        part = pl.ds(c * each * order, each * order)
        started.append(pltpu.make_async_copy(rows.at[:, part], out.at[:, part], sent.at[c]))
        started[c].start()
    for copy in started:
        copy.wait()


def unpack(place, arrived):
    _, strip, width = arrived.shape
    columns = place.shape[1] * (width // 3)
    return pl.pallas_call(
        unpack_kernel,
        in_specs=[pl.BlockSpec(memory_space=pltpu.SMEM), pl.BlockSpec(memory_space=pltpu.VMEM)],
        out_specs=pl.BlockSpec(memory_space=pltpu.HBM),
        out_shape=jax.ShapeDtypeStruct((strip, columns), jnp.bfloat16),
        scratch_shapes=[pltpu.VMEM((strip, columns), jnp.bfloat16), pltpu.SemaphoreType.DMA((4,))],
        compiler_params=pltpu.CompilerParams(vmem_limit_bytes=16 * 2**20),
    )(place, arrived)


def start_half(which, partial, out, copied):
    pieces = copied.shape[0]
    columns = out.shape[1] // pieces
    copies = []
    for i in range(pieces):
        at = pl.ds(pl.multiple_of((which * pieces + i) * columns, columns), columns)
        copies.append(
            pltpu.make_async_copy(
                partial.at[:, at], out.at[:, i * columns : (i + 1) * columns], copied.at[i]
            )
        )
        copies[i].start()
    return copies


def leave_kernel(partial, out, copied):
    for copy in start_half(1 - lax.axis_index("replica"), partial, out, copied):
        copy.wait()


def leaving_half(partial):
    rows, columns = partial.shape
    return pl.pallas_call(
        leave_kernel,
        in_specs=[pl.BlockSpec(memory_space=pltpu.HBM)],
        out_specs=pl.BlockSpec(memory_space=pltpu.VMEM),
        out_shape=pltpu.VMEM((rows, columns // 2), partial.dtype),
        scratch_shapes=[pltpu.SemaphoreType.DMA((4,))],
        compiler_params=pltpu.CompilerParams(vmem_limit_bytes=8 * 2**20),
    )(pltpu.with_memory_space_constraint(partial, pltpu.HBM))


def stay_kernel(partial, owners, out, source, place, load, copied, *, slots):
    half = lax.axis_index("replica")
    copies = start_half(half, partial, out, copied)
    blocks = owners.shape[1]
    square = (blocks, blocks)
    both = owners[...].astype(jnp.float32)
    along = jnp.where(half == 0, both[0:1], both[1:2])
    owner_of_lane = jnp.broadcast_to(along, square)
    owner_of_row = owner_of_lane.T
    row, lane = lax.broadcasted_iota(jnp.int32, square, 0), lax.broadcasted_iota(jnp.int32, square, 1)
    same = owner_of_lane == owner_of_row
    rank_of_lane = jnp.sum(jnp.where(same & (row < lane), 1.0, 0.0), axis=0, keepdims=True)
    rank_of_row = jnp.sum(jnp.where(same & (lane < row), 1.0, 0.0), axis=1, keepdims=True)
    target = owner_of_row[:, 0:1] * slots + rank_of_row
    wide = (blocks, source.shape[1])
    slot = lax.broadcasted_iota(jnp.int32, wide, 1).astype(jnp.float32)
    block = lax.broadcasted_iota(jnp.int32, wide, 0).astype(jnp.float32)
    named = jnp.where(jnp.broadcast_to(target, wide) == slot, block, 0.0)
    source[...] = jnp.sum(named, axis=0, keepdims=True).astype(jnp.int32)
    place[...] = jnp.concatenate([along, rank_of_lane], axis=0).astype(jnp.int32)
    mine = lax.axis_index("fsdp").astype(jnp.float32)
    loads = jnp.sum(jnp.where(along == mine, 1.0, 0.0), axis=1, keepdims=True)
    load[...] = jnp.broadcast_to(loads, load.shape).astype(jnp.int32)
    for copy in copies:
        copy.wait()


def staying_half(partial, owners, destinations, slots):
    rows, columns = partial.shape
    blocks = owners.shape[1]
    near = pl.BlockSpec(memory_space=pltpu.VMEM)
    lanes = -(-destinations * slots // 128) * 128
    return pl.pallas_call(
        functools.partial(stay_kernel, slots=slots),
        in_specs=[pl.BlockSpec(memory_space=pltpu.HBM), near],
        out_specs=[near] * 4,
        out_shape=[
            pltpu.VMEM((rows, columns // 2), partial.dtype),
            jax.ShapeDtypeStruct((1, lanes), jnp.int32),
            jax.ShapeDtypeStruct((2, blocks), jnp.int32),
            jax.ShapeDtypeStruct((1, 128), jnp.int32),
        ],
        scratch_shapes=[pltpu.SemaphoreType.DMA((4,))],
        compiler_params=pltpu.CompilerParams(vmem_limit_bytes=8 * 2**20),
    )(pltpu.with_memory_space_constraint(partial, pltpu.HBM), owners)


def shards(partials, owners, left_stat, right_stat, left_root, right_root, second_moment):
    fsdp_count = lax.axis_size("fsdp")
    slots, order, _ = left_stat.shape
    strip = partials.shape[1]
    partial = partials[0]
    theirs = lax.ppermute(leaving_half(partial), "replica", [(0, 1), (1, 0)])
    mine, source, place, load = staying_half(partial, owners[:, :, 0], fsdp_count, slots)
    outgoing = pack(source, mine, theirs, fsdp_count, slots, order)
    grads = lax.all_to_all(outgoing, "fsdp", split_axis=0, concat_axis=0, tiled=True)
    fresh = updates(grads, left_root, right_root, second_moment)
    arrived = lax.all_to_all(fresh, "fsdp", split_axis=0, concat_axis=0, tiled=True)
    left_next, right_next, moment_next = states(load, grads, left_stat, right_stat, second_moment)
    update = unpack(place, arrived.reshape(fsdp_count, strip, slots * order))
    return (left_next, right_next, moment_next, update)


def solution(mesh):
    placed = (
        P("replica", "fsdp", None),
        P(),
        P(("replica", "fsdp"), None, None),
        P(("replica", "fsdp"), None, None),
        P(("replica", "fsdp"), None, None),
        P(("replica", "fsdp"), None, None),
        P(("replica", "fsdp"), None, None),
    )
    return jax.shard_map(
        shards,
        mesh=mesh,
        in_specs=placed,
        out_specs=(
            P(("replica", "fsdp"), None, None),
            P(("replica", "fsdp"), None, None),
            P(("replica", "fsdp"), None, None),
            P("fsdp", "replica"),
        ),
        check_vma=False,
    )
```

```python
import functools

import jax
import jax.numpy as jnp
from jax import lax
from jax.experimental import pallas as pl
from jax.experimental.pallas import tpu as pltpu
from jax.sharding import PartitionSpec as P

FACTOR_DECAY = 0.9
MOMENT_DECAY = 0.99

GRADS_ORDER = 62
UPDATE_ORDER = 42
PAIR = 16


def group(order, count):
    return [[i ^ order for i in range(count)]]


def in_rows(grads, columns, first, last):
    pairs = [PAIR * (p ^ (GRADS_ORDER // 2)) for p in range(first // PAIR, last // PAIR)]
    return jnp.concatenate([grads[p : p + PAIR, columns] for p in pairs], axis=0)


def pack_kernel(source, mine, theirs, out):
    strip, order = 8, out.shape[1] // 3

    def summed(block):
        at = pl.ds(pl.multiple_of(block * order, order), order)
        return mine[:, at].astype(jnp.float32) + theirs[:, at].astype(jnp.float32)

    def step(i, carry):
        for q in range(3):
            pair = [summed(source[0, (2 * i + j) * 3 + q]) for j in range(2)]
            rows = pl.ds(pl.multiple_of(i * 2 * strip, 2 * strip), 2 * strip)
            out[rows, q * order : (q + 1) * order] = jnp.concatenate(pair, axis=0).astype(out.dtype)
        return carry

    lax.fori_loop(0, out.shape[0] // (2 * strip), step, 0, unroll=4)


def pack(source, mine, theirs, destinations, slots, order):
    few, near = pl.BlockSpec(memory_space=pltpu.SMEM), pl.BlockSpec(memory_space=pltpu.VMEM)
    return pl.pallas_call(
        pack_kernel,
        in_specs=[few, near, near],
        out_specs=near,
        out_shape=jax.ShapeDtypeStruct((destinations * mine.shape[0], slots * order), jnp.bfloat16),
        compiler_params=pltpu.CompilerParams(vmem_limit_bytes=16 * 2**20),
    )(source, mine, theirs)


def update_kernel(grads, root_left, root_right, moment, out, half_way, shampoo, result, sent):
    slots, order, _ = moment.shape
    parts, count = sent.shape[1], float(order * order)

    def folded(square):
        return jnp.sum(square.reshape(-1, 8, order), axis=0)

    def columns(s):
        return slice(s * order, (s + 1) * order)

    def rows_of(part, of=parts):
        return slice(part * order // of, (part + 1) * order // of)

    zero = jnp.zeros((8, order), jnp.float32)
    adam_square = [zero] * slots
    chunks = [(s, i) for s in range(slots) for i in range(16)]
    each = len(chunks) // (slots * parts)
    for step in range(slots * parts):
        s, rows = step // parts, rows_of(step % parts)
        block = in_rows(grads, columns(s), 0, order)
        left = jnp.dot(root_left[s, rows], block, preferred_element_type=jnp.float32)
        half_way[s, rows] = left.astype(half_way.dtype)
        for r, i in chunks[step * each : (step + 1) * each]:
            some = rows_of(i, 16)
            g = in_rows(grads, columns(r), some.start, some.stop).astype(jnp.float32)
            fresh = MOMENT_DECAY * moment[r, some] + (1.0 - MOMENT_DECAY) * g * g
            adam = g / (fresh * lax.rsqrt(fresh) + 1e-08)
            adam_square[r] = adam_square[r] + folded(adam * adam)
    copies = []
    for s in range(slots):
        shampoo_square = zero
        for part in range(parts):
            rows = rows_of(part)
            both = jnp.dot(half_way[s, rows], root_right[s], preferred_element_type=jnp.float32)
            shampoo[s, rows] = both
            shampoo_square = shampoo_square + folded(both * both)
        scale = jnp.sqrt(jnp.sum(adam_square[s]) / count) / jnp.sqrt(
            jnp.sum(shampoo_square) / count + 1e-06
        )
        for part in range(parts):
            rows = rows_of(part)
            for place in range(rows.start, rows.stop, PAIR):
                row = PAIR * ((place // PAIR) ^ (UPDATE_ORDER // 2))
                piece = shampoo[s, row : row + PAIR] * scale
                result[s, place : place + PAIR] = piece.astype(result.dtype)
            copies.append(
                pltpu.make_async_copy(
                    result.at[s, rows], out.at[rows, columns(s)], sent.at[s, part]
                )
            )
            copies[-1].start()
    for copy in copies:
        copy.wait()


def updates(grads, root_left, root_right, moment):
    slots, order, _ = moment.shape
    near = pl.BlockSpec(memory_space=pltpu.VMEM)
    return pl.pallas_call(
        update_kernel,
        in_specs=[near] * 4,
        out_specs=pl.BlockSpec(memory_space=pltpu.HBM),
        out_shape=pltpu.HBM(grads.shape, jnp.bfloat16),
        scratch_shapes=[
            pltpu.VMEM((slots, order, order), jnp.bfloat16),
            pltpu.VMEM((slots, order, order), jnp.float32),
            pltpu.VMEM((slots, order, order), jnp.bfloat16),
            pltpu.SemaphoreType.DMA((slots, 4)),
        ],
        compiler_params=pltpu.CompilerParams(vmem_limit_bytes=24 * 2**20),
    )(grads, root_left, root_right, moment)


def state_kernel(load, grad, left, right, moment, left_out, right_out, moment_out):
    active = pl.program_id(0) < load[0, 0]

    @pl.when(active)
    def _():
        g = in_rows(grad, slice(None), 0, grad.shape[0])
        weight = (1.0 - FACTOR_DECAY) / g.shape[0]
        gram = lax.dot_general(g, g, (((1,), (1,)), ((), ())), preferred_element_type=jnp.float32)
        left_out[0] = FACTOR_DECAY * left[0] + weight * gram
        gram = lax.dot_general(g, g, (((0,), (0,)), ((), ())), preferred_element_type=jnp.float32)
        right_out[0] = FACTOR_DECAY * right[0] + weight * gram
        g = g.astype(jnp.float32)
        moment_out[0] = MOMENT_DECAY * moment[0] + (1.0 - MOMENT_DECAY) * g * g

    @pl.when(jnp.logical_not(active))
    def _():
        left_out[...] = left[...]
        right_out[...] = right[...]
        moment_out[...] = moment[...]


def states(load, grads, left, right, moment):
    slots, order, _ = moment.shape
    slot = pl.BlockSpec((1, order, order), lambda s, load: (s, 0, 0))
    columns = pl.BlockSpec((order, order), lambda s, load: (0, s))
    kept = jax.ShapeDtypeStruct(moment.shape, jnp.float32)
    return pl.pallas_call(
        state_kernel,
        grid_spec=pltpu.PrefetchScalarGridSpec(
            num_scalar_prefetch=1,
            grid=(slots,),
            in_specs=[columns, slot, slot, slot],
            out_specs=[slot, slot, slot],
        ),
        out_shape=[kept, kept, kept],
        compiler_params=pltpu.CompilerParams(vmem_limit_bytes=32 * 2**20),
        cost_estimate=pl.CostEstimate(
            flops=4 * slots * order**3, bytes_accessed=26 * slots * order**2, transcendentals=0
        ),
    )(load, grads, left, right, moment)


def unpack_kernel(place, arrived, out, rows, sent):
    order = arrived.shape[2] // 3
    blocks, copies = place.shape[1], sent.shape[0]
    each = blocks // copies
    started = []
    for c in range(copies):

        def step(i, carry):
            k = c * each + i
            at = pl.ds(pl.multiple_of(place[1, k] * order, order), order)
            to = pl.ds(pl.multiple_of(k * order, order), order)
            rows[:, to] = arrived[place[0, k], :, at]
            return carry

        lax.fori_loop(0, each, step, 0, unroll=True)
        part = pl.ds(c * each * order, each * order)
        started.append(pltpu.make_async_copy(rows.at[:, part], out.at[:, part], sent.at[c]))
        started[c].start()
    for copy in started:
        copy.wait()


def unpack(place, arrived):
    _, strip, width = arrived.shape
    columns = place.shape[1] * (width // 3)
    return pl.pallas_call(
        unpack_kernel,
        in_specs=[pl.BlockSpec(memory_space=pltpu.SMEM), pl.BlockSpec(memory_space=pltpu.VMEM)],
        out_specs=pl.BlockSpec(memory_space=pltpu.HBM),
        out_shape=jax.ShapeDtypeStruct((strip, columns), jnp.bfloat16),
        scratch_shapes=[pltpu.VMEM((strip, columns), jnp.bfloat16), pltpu.SemaphoreType.DMA((4,))],
        compiler_params=pltpu.CompilerParams(vmem_limit_bytes=16 * 2**20),
    )(place, arrived)


def start_half(which, partial, out, copied):
    pieces = copied.shape[0]
    columns = out.shape[1] // pieces
    copies = []
    for i in range(pieces):
        at = pl.ds(pl.multiple_of((which * pieces + i) * columns, columns), columns)
        copies.append(
            pltpu.make_async_copy(
                partial.at[:, at], out.at[:, i * columns : (i + 1) * columns], copied.at[i]
            )
        )
        copies[i].start()
    return copies


def leave_kernel(partial, out, copied):
    for copy in start_half(1 - lax.axis_index("replica"), partial, out, copied):
        copy.wait()


def leaving_half(partial):
    rows, columns = partial.shape
    return pl.pallas_call(
        leave_kernel,
        in_specs=[pl.BlockSpec(memory_space=pltpu.HBM)],
        out_specs=pl.BlockSpec(memory_space=pltpu.VMEM),
        out_shape=pltpu.VMEM((rows, columns // 2), partial.dtype),
        scratch_shapes=[pltpu.SemaphoreType.DMA((4,))],
        compiler_params=pltpu.CompilerParams(vmem_limit_bytes=8 * 2**20),
    )(pltpu.with_memory_space_constraint(partial, pltpu.HBM))


def stay_kernel(partial, owners, out, source, place, load, copied, *, slots):
    half = lax.axis_index("replica")
    copies = start_half(half, partial, out, copied)
    blocks = owners.shape[1]
    square = (blocks, blocks)
    both = owners[...]
    along = jnp.where(half == 0, both[0:1], both[1:2])
    owner_of_lane = jnp.broadcast_to((along ^ GRADS_ORDER).astype(jnp.float32), square)
    owner_of_row = owner_of_lane.T
    row, lane = lax.broadcasted_iota(jnp.int32, square, 0), lax.broadcasted_iota(jnp.int32, square, 1)
    same = owner_of_lane == owner_of_row
    rank_of_lane = jnp.sum(jnp.where(same & (row < lane), 1.0, 0.0), axis=0, keepdims=True)
    rank_of_row = jnp.sum(jnp.where(same & (lane < row), 1.0, 0.0), axis=1, keepdims=True)
    target = owner_of_row[:, 0:1] * slots + rank_of_row
    wide = (blocks, source.shape[1])
    slot = lax.broadcasted_iota(jnp.int32, wide, 1).astype(jnp.float32)
    block = lax.broadcasted_iota(jnp.int32, wide, 0).astype(jnp.float32)
    named = jnp.where(jnp.broadcast_to(target, wide) == slot, block, 0.0)
    source[...] = jnp.sum(named, axis=0, keepdims=True).astype(jnp.int32)
    place[...] = jnp.concatenate([along ^ UPDATE_ORDER, rank_of_lane.astype(jnp.int32)], axis=0)
    loads = jnp.sum(jnp.where(along == lax.axis_index("fsdp"), 1.0, 0.0), axis=1, keepdims=True)
    load[...] = jnp.broadcast_to(loads, load.shape).astype(jnp.int32)
    for copy in copies:
        copy.wait()


def staying_half(partial, owners, destinations, slots):
    rows, columns = partial.shape
    blocks = owners.shape[1]
    near = pl.BlockSpec(memory_space=pltpu.VMEM)
    lanes = -(-destinations * slots // 128) * 128
    return pl.pallas_call(
        functools.partial(stay_kernel, slots=slots),
        in_specs=[pl.BlockSpec(memory_space=pltpu.HBM), near],
        out_specs=[near] * 4,
        out_shape=[
            pltpu.VMEM((rows, columns // 2), partial.dtype),
            jax.ShapeDtypeStruct((1, lanes), jnp.int32),
            jax.ShapeDtypeStruct((2, blocks), jnp.int32),
            jax.ShapeDtypeStruct((1, 128), jnp.int32),
        ],
        scratch_shapes=[pltpu.SemaphoreType.DMA((4,))],
        compiler_params=pltpu.CompilerParams(vmem_limit_bytes=8 * 2**20),
    )(pltpu.with_memory_space_constraint(partial, pltpu.HBM), owners)


def shards(partials, owners, left_stat, right_stat, left_root, right_root, second_moment):
    fsdp_count = lax.axis_size("fsdp")
    slots, order, _ = left_stat.shape
    strip = partials.shape[1]
    partial = partials[0]
    theirs = lax.ppermute(leaving_half(partial), "replica", [(0, 1), (1, 0)])
    mine, source, place, load = staying_half(partial, owners[:, :, 0], fsdp_count, slots)
    outgoing = pack(source, mine, theirs, fsdp_count, slots, order)
    exchange = functools.partial(
        lax.all_to_all, axis_name="fsdp", split_axis=0, concat_axis=0, tiled=True
    )
    grads = exchange(outgoing, axis_index_groups=group(GRADS_ORDER, fsdp_count))
    fresh = updates(grads, left_root, right_root, second_moment)
    arrived = exchange(fresh, axis_index_groups=group(UPDATE_ORDER, fsdp_count))
    left_next, right_next, moment_next = states(load, grads, left_stat, right_stat, second_moment)
    update = unpack(place, arrived.reshape(fsdp_count, strip, slots * order))
    return (left_next, right_next, moment_next, update)


def solution(mesh):
    placed = (
        P("replica", "fsdp", None),
        P(),
        P(("replica", "fsdp"), None, None),
        P(("replica", "fsdp"), None, None),
        P(("replica", "fsdp"), None, None),
        P(("replica", "fsdp"), None, None),
        P(("replica", "fsdp"), None, None),
    )
    return jax.shard_map(
        shards,
        mesh=mesh,
        in_specs=placed,
        out_specs=(
            P(("replica", "fsdp"), None, None),
            P(("replica", "fsdp"), None, None),
            P(("replica", "fsdp"), None, None),
            P("fsdp", "replica"),
        ),
        check_vma=False,
    )
```

```python
import functools

import jax
import jax.numpy as jnp
from jax import lax
from jax.experimental import pallas as pl
from jax.experimental.pallas import tpu as pltpu
from jax.sharding import PartitionSpec as P

FACTOR_DECAY = 0.9
MOMENT_DECAY = 0.99

GRADS_ORDER = 58
UPDATE_ORDER = 42
PAIR = 16


def group(order, count):
    return [[i ^ order for i in range(count)]]


def in_rows(grads, columns, first, last):
    pairs = [PAIR * (p ^ (GRADS_ORDER // 2)) for p in range(first // PAIR, last // PAIR)]
    return jnp.concatenate([grads[p : p + PAIR, columns] for p in pairs], axis=0)


def pack_kernel(source, mine, theirs, out):
    strip, order = 8, out.shape[1] // 3

    def summed(block):
        at = pl.ds(pl.multiple_of(block * order, order), order)
        return mine[:, at].astype(jnp.float32) + theirs[:, at].astype(jnp.float32)

    def step(i, carry):
        for q in range(3):
            pair = [summed(source[0, (2 * i + j) * 3 + q]) for j in range(2)]
            rows = pl.ds(pl.multiple_of(i * 2 * strip, 2 * strip), 2 * strip)
            out[rows, q * order : (q + 1) * order] = jnp.concatenate(pair, axis=0).astype(out.dtype)
        return carry

    lax.fori_loop(0, out.shape[0] // (2 * strip), step, 0, unroll=4)


def pack(source, mine, theirs, destinations, slots, order):
    few, near = pl.BlockSpec(memory_space=pltpu.SMEM), pl.BlockSpec(memory_space=pltpu.VMEM)
    return pl.pallas_call(
        pack_kernel,
        in_specs=[few, near, near],
        out_specs=near,
        out_shape=jax.ShapeDtypeStruct((destinations * mine.shape[0], slots * order), jnp.bfloat16),
        compiler_params=pltpu.CompilerParams(vmem_limit_bytes=16 * 2**20),
    )(source, mine, theirs)


def update_kernel(grads, root_left, root_right, moment, out, half_way, shampoo, result, sent):
    slots, order, _ = moment.shape
    parts, count = sent.shape[1], float(order * order)

    def folded(square):
        return jnp.sum(square.reshape(-1, 8, order), axis=0)

    def columns(s):
        return slice(s * order, (s + 1) * order)

    def rows_of(part, of=parts):
        return slice(part * order // of, (part + 1) * order // of)

    zero = jnp.zeros((8, order), jnp.float32)
    adam_square = [zero] * slots
    chunks = [(s, i) for s in range(slots) for i in range(16)]
    each = len(chunks) // (slots * parts)
    for step in range(slots * parts):
        s, rows = step // parts, rows_of(step % parts)
        block = in_rows(grads, columns(s), 0, order)
        left = jnp.dot(root_left[s, rows], block, preferred_element_type=jnp.float32)
        half_way[s, rows] = left.astype(half_way.dtype)
        for r, i in chunks[step * each : (step + 1) * each]:
            some = rows_of(i, 16)
            g = in_rows(grads, columns(r), some.start, some.stop).astype(jnp.float32)
            fresh = MOMENT_DECAY * moment[r, some] + (1.0 - MOMENT_DECAY) * g * g
            adam = g / (fresh * lax.rsqrt(fresh) + 1e-08)
            adam_square[r] = adam_square[r] + folded(adam * adam)
    copies = []
    for s in range(slots):
        shampoo_square = zero
        for part in range(parts):
            rows = rows_of(part)
            right = jnp.concatenate([root_right[s, i : i + 64] for i in range(0, order, 64)], axis=0)
            both = jnp.dot(half_way[s, rows], right, preferred_element_type=jnp.float32)
            shampoo[s, rows] = both
            shampoo_square = shampoo_square + folded(both * both)
        scale = jnp.sqrt(jnp.sum(adam_square[s]) / count) / jnp.sqrt(
            jnp.sum(shampoo_square) / count + 1e-06
        )
        for part in range(parts):
            rows = rows_of(part)
            for place in range(rows.start, rows.stop, PAIR):
                row = PAIR * ((place // PAIR) ^ (UPDATE_ORDER // 2))
                piece = shampoo[s, row : row + PAIR] * scale
                result[s, place : place + PAIR] = piece.astype(result.dtype)
            copies.append(
                pltpu.make_async_copy(
                    result.at[s, rows], out.at[rows, columns(s)], sent.at[s, part]
                )
            )
            copies[-1].start()
    for copy in copies:
        copy.wait()


def updates(grads, root_left, root_right, moment):
    slots, order, _ = moment.shape
    near = pl.BlockSpec(memory_space=pltpu.VMEM)
    return pl.pallas_call(
        update_kernel,
        in_specs=[near] * 4,
        out_specs=pl.BlockSpec(memory_space=pltpu.HBM),
        out_shape=pltpu.HBM(grads.shape, jnp.bfloat16),
        scratch_shapes=[
            pltpu.VMEM((slots, order, order), jnp.bfloat16),
            pltpu.VMEM((slots, order, order), jnp.float32),
            pltpu.VMEM((slots, order, order), jnp.bfloat16),
            pltpu.SemaphoreType.DMA((slots, 4)),
        ],
        compiler_params=pltpu.CompilerParams(vmem_limit_bytes=24 * 2**20),
    )(grads, root_left, root_right, moment)


def state_kernel(load, grad, left, right, moment, left_out, right_out, moment_out):
    active = pl.program_id(0) < load[0, 0]

    @pl.when(active)
    def _():
        g = in_rows(grad, slice(None), 0, grad.shape[0])
        weight = (1.0 - FACTOR_DECAY) / g.shape[0]
        gram = lax.dot_general(g, g, (((1,), (1,)), ((), ())), preferred_element_type=jnp.float32)
        left_out[0] = FACTOR_DECAY * left[0] + weight * gram
        gram = lax.dot_general(g, g, (((0,), (0,)), ((), ())), preferred_element_type=jnp.float32)
        right_out[0] = FACTOR_DECAY * right[0] + weight * gram
        g = g.astype(jnp.float32)
        moment_out[0] = MOMENT_DECAY * moment[0] + (1.0 - MOMENT_DECAY) * g * g

    @pl.when(jnp.logical_not(active))
    def _():
        left_out[...] = left[...]
        right_out[...] = right[...]
        moment_out[...] = moment[...]


def states(load, grads, left, right, moment):
    slots, order, _ = moment.shape
    slot = pl.BlockSpec((1, order, order), lambda s, load: (s, 0, 0))
    columns = pl.BlockSpec((order, order), lambda s, load: (0, s))
    kept = jax.ShapeDtypeStruct(moment.shape, jnp.float32)
    return pl.pallas_call(
        state_kernel,
        grid_spec=pltpu.PrefetchScalarGridSpec(
            num_scalar_prefetch=1,
            grid=(slots,),
            in_specs=[columns, slot, slot, slot],
            out_specs=[slot, slot, slot],
        ),
        out_shape=[kept, kept, kept],
        compiler_params=pltpu.CompilerParams(vmem_limit_bytes=32 * 2**20),
        cost_estimate=pl.CostEstimate(
            flops=4 * slots * order**3, bytes_accessed=26 * slots * order**2, transcendentals=0
        ),
    )(load, grads, left, right, moment)


def unpack_kernel(place, arrived, out, rows, sent):
    order = arrived.shape[2] // 3
    blocks, copies = place.shape[1], sent.shape[0]
    each = blocks // copies
    started = []
    for c in range(copies):

        def step(i, carry):
            k = c * each + i
            at = pl.ds(pl.multiple_of(place[1, k] * order, order), order)
            to = pl.ds(pl.multiple_of(k * order, order), order)
            rows[:, to] = arrived[place[0, k], :, at]
            return carry

        lax.fori_loop(0, each, step, 0, unroll=True)
        part = pl.ds(c * each * order, each * order)
        started.append(pltpu.make_async_copy(rows.at[:, part], out.at[:, part], sent.at[c]))
        started[c].start()
    for copy in started:
        copy.wait()


def unpack(place, arrived):
    _, strip, width = arrived.shape
    columns = place.shape[1] * (width // 3)
    return pl.pallas_call(
        unpack_kernel,
        in_specs=[pl.BlockSpec(memory_space=pltpu.SMEM), pl.BlockSpec(memory_space=pltpu.VMEM)],
        out_specs=pl.BlockSpec(memory_space=pltpu.HBM),
        out_shape=jax.ShapeDtypeStruct((strip, columns), jnp.bfloat16),
        scratch_shapes=[pltpu.VMEM((strip, columns), jnp.bfloat16), pltpu.SemaphoreType.DMA((4,))],
        compiler_params=pltpu.CompilerParams(vmem_limit_bytes=16 * 2**20),
    )(place, arrived)


def start_half(which, partial, out, copied):
    pieces = copied.shape[0]
    columns = out.shape[1] // pieces
    copies = []
    for i in range(pieces):
        at = pl.ds(pl.multiple_of((which * pieces + i) * columns, columns), columns)
        copies.append(
            pltpu.make_async_copy(
                partial.at[:, at], out.at[:, i * columns : (i + 1) * columns], copied.at[i]
            )
        )
        copies[i].start()
    return copies


def leave_kernel(partial, out, copied):
    for copy in start_half(1 - lax.axis_index("replica"), partial, out, copied):
        copy.wait()


def leaving_half(partial):
    rows, columns = partial.shape
    return pl.pallas_call(
        leave_kernel,
        in_specs=[pl.BlockSpec(memory_space=pltpu.HBM)],
        out_specs=pl.BlockSpec(memory_space=pltpu.VMEM),
        out_shape=pltpu.VMEM((rows, columns // 2), partial.dtype),
        scratch_shapes=[pltpu.SemaphoreType.DMA((4,))],
        compiler_params=pltpu.CompilerParams(vmem_limit_bytes=8 * 2**20),
    )(pltpu.with_memory_space_constraint(partial, pltpu.HBM))


def stay_kernel(partial, owners, out, source, place, load, copied, *, slots):
    half = lax.axis_index("replica")
    copies = start_half(half, partial, out, copied)
    blocks = owners.shape[1]
    square = (blocks, blocks)
    both = owners[...]
    along = jnp.where(half == 0, both[0:1], both[1:2])
    owner_of_lane = jnp.broadcast_to((along ^ GRADS_ORDER).astype(jnp.float32), square)
    owner_of_row = owner_of_lane.T
    row, lane = lax.broadcasted_iota(jnp.int32, square, 0), lax.broadcasted_iota(jnp.int32, square, 1)
    same = owner_of_lane == owner_of_row
    rank_of_lane = jnp.sum(jnp.where(same & (row < lane), 1.0, 0.0), axis=0, keepdims=True)
    rank_of_row = jnp.sum(jnp.where(same & (lane < row), 1.0, 0.0), axis=1, keepdims=True)
    target = owner_of_row[:, 0:1] * slots + rank_of_row
    wide = (blocks, source.shape[1])
    slot = lax.broadcasted_iota(jnp.int32, wide, 1).astype(jnp.float32)
    block = lax.broadcasted_iota(jnp.int32, wide, 0).astype(jnp.float32)
    named = jnp.where(jnp.broadcast_to(target, wide) == slot, block, 0.0)
    source[...] = jnp.sum(named, axis=0, keepdims=True).astype(jnp.int32)
    place[...] = jnp.concatenate([along ^ UPDATE_ORDER, rank_of_lane.astype(jnp.int32)], axis=0)
    loads = jnp.sum(jnp.where(along == lax.axis_index("fsdp"), 1.0, 0.0), axis=1, keepdims=True)
    load[...] = jnp.broadcast_to(loads, load.shape).astype(jnp.int32)
    for copy in copies:
        copy.wait()


def staying_half(partial, owners, destinations, slots):
    rows, columns = partial.shape
    blocks = owners.shape[1]
    near = pl.BlockSpec(memory_space=pltpu.VMEM)
    lanes = -(-destinations * slots // 128) * 128
    return pl.pallas_call(
        functools.partial(stay_kernel, slots=slots),
        in_specs=[pl.BlockSpec(memory_space=pltpu.HBM), near],
        out_specs=[near] * 4,
        out_shape=[
            pltpu.VMEM((rows, columns // 2), partial.dtype),
            jax.ShapeDtypeStruct((1, lanes), jnp.int32),
            jax.ShapeDtypeStruct((2, blocks), jnp.int32),
            jax.ShapeDtypeStruct((1, 128), jnp.int32),
        ],
        scratch_shapes=[pltpu.SemaphoreType.DMA((4,))],
        compiler_params=pltpu.CompilerParams(vmem_limit_bytes=8 * 2**20),
    )(pltpu.with_memory_space_constraint(partial, pltpu.HBM), owners)


def shards(partials, owners, left_stat, right_stat, left_root, right_root, second_moment):
    fsdp_count = lax.axis_size("fsdp")
    slots, order, _ = left_stat.shape
    strip = partials.shape[1]
    partial = partials[0]
    theirs = lax.ppermute(leaving_half(partial), "replica", [(0, 1), (1, 0)])
    mine, source, place, load = staying_half(partial, owners[:, :, 0], fsdp_count, slots)
    outgoing = pack(source, mine, theirs, fsdp_count, slots, order)
    exchange = functools.partial(
        lax.all_to_all, axis_name="fsdp", split_axis=0, concat_axis=0, tiled=True
    )
    grads = exchange(outgoing, axis_index_groups=group(GRADS_ORDER, fsdp_count))
    fresh = updates(grads, left_root, right_root, second_moment)
    arrived = exchange(fresh, axis_index_groups=group(UPDATE_ORDER, fsdp_count))
    left_next, right_next, moment_next = states(load, grads, left_stat, right_stat, second_moment)
    update = unpack(place, arrived.reshape(fsdp_count, strip, slots * order))
    return (left_next, right_next, moment_next, update)


def solution(mesh):
    placed = (
        P("replica", "fsdp", None),
        P(),
        P(("replica", "fsdp"), None, None),
        P(("replica", "fsdp"), None, None),
        P(("replica", "fsdp"), None, None),
        P(("replica", "fsdp"), None, None),
        P(("replica", "fsdp"), None, None),
    )
    return jax.shard_map(
        shards,
        mesh=mesh,
        in_specs=placed,
        out_specs=(
            P(("replica", "fsdp"), None, None),
            P(("replica", "fsdp"), None, None),
            P(("replica", "fsdp"), None, None),
            P("fsdp", "replica"),
        ),
        check_vma=False,
    )
```
